256 devices in a mesh: rep: 8 (over z_hi, core), fsdp: 16 (over y, x), tp: 2 (over z_lo).
Axes of the slice: x: 4, y: 4, z: 8 (z_hi: 4, z_lo: 2; z = z_hi * 2 + z_lo), core: 2. Of those that a mesh axis runs over, the one named last changes fastest.
Arguments:
- queries: bfloat16 [4, 512, 8192], P(None, ('rep', 'fsdp'), 'tp'), may hold values from -512 to 512
- cache_keys: bfloat16 [512, 1024, 512], P(('rep', 'fsdp'), None, 'tp'), may hold values from -5 to 5
- cache_values: bfloat16 [512, 1024, 512], P(('rep', 'fsdp'), None, 'tp'), may hold values from -6 to 6
- new_keys: bfloat16 [4, 512, 512], P(None, ('rep', 'fsdp'), 'tp'), may hold values from -6 to 6
- new_values: bfloat16 [4, 512, 512], P(None, ('rep', 'fsdp'), 'tp'), may hold values from -6 to 6
- lengths: int32 [512], P(('rep', 'fsdp')), may hold values from 64 to 1024, as said below
- attn_out_weight: bfloat16 [8192, 4096], P(('tp', 'rep'), 'fsdp'), may hold values from -0.125 to 0.125
- residual: bfloat16 [4, 512, 4096], P(None, 'rep', 'fsdp'), may hold values from -6 to 6
- norm_gain: float32 [4096], P('fsdp'), may hold values from 0.1 to 1.9
- expert_ids: int32 [4, 512, 8], P(None, 'rep'), may hold values from 0 to 15, all different within a row; in each aligned block of 64 rows (0 to 63, 64 to 127, ..., all dimensions but the last counted through in order) at most 48 rows name the same one
- gate_weights: bfloat16 [4, 512, 8], P(None, 'rep'), may hold values from 0.049804688 to 0.34960938
- expert_in: bfloat16 [16, 4096, 2, 1536], P('fsdp', 'rep', None, 'tp'), may hold values from -0.09375 to 0.09375
- expert_out: bfloat16 [16, 1536, 4096], P('fsdp', 'tp', 'rep'), may hold values from -0.15625 to 0.15625
Outputs:
- layer_out: bfloat16 [4, 512, 4096], P(None, 'rep', 'fsdp')
The draws below stay inside these ranges and needn't reach their ends.
Inputs may be any that keep to these rules, and one draw needn't show every extreme that they name: `expert_ids`: each row names 8 different experts; in each aligned block of 64 rows (one step of one replica) no expert is named by more than 48 rows. `lengths`: some sequence has exactly 1024 filled positions.
All inputs are finite; a program needn't handle non-finite values.
Results may differ from the reference program's by a relative error of at most 0.0055.
Values may be sent and summed in bfloat16 or wider, within the bound.
No kernel may reach another device: no remote copies, remote signals or barrier semaphores. Data moves between devices by JAX's collectives and lax.ppermute only.
A program may use at most 128 MiB of HBM per device.

```python
import math
import jax
import jax.numpy as jnp
import numpy as np
from jax import lax

D = 4096
FF = 1536
HQ = 64
KVH = 4
HD = 128
ROW_DEV = 4
CACHE = 1024
STEPS = 4
ROWS = 512
BLOCK = 64
EXPERTS = 16
TOPK = 8
CAP = 48


def shared_keys(key):
    common = jax.random.normal(jax.random.fold_in(key, 77), (ROWS, CACHE, KVH * HD), jnp.float32)
    return jnp.clip(common, -5.0, 5.0)


def draw_cache_keys(key, part):
    common = shared_keys(key)
    return common.astype(jnp.bfloat16)


def draw_queries(key, part):
    key = jax.random.fold_in(key, 12)
    key_drawn = jax.random.fold_in(key, 0)
    shape = (STEPS, ROWS, HQ * HD)
    entries = jax.random.normal(key_drawn, shape, jnp.float32)
    return jnp.clip(entries, -6.0, 6.0).astype(jnp.bfloat16)


def draw_lengths(key, part):
    key = jax.random.fold_in(key, 13)
    key_lengths, key_full = jax.random.split(key, 2)
    lowest = max(2, CACHE // 16)
    drawn = jax.random.randint(key_lengths, (ROWS,), lowest, CACHE + 1)
    full_row = jax.random.randint(key_full, (), 0, ROWS)
    return jnp.where(jnp.arange(ROWS) == full_row, CACHE, drawn).astype(jnp.int32)


def draw_residual(key, part):
    key = jax.random.fold_in(key, 14)
    key_values, key_quiet = jax.random.split(key, 2)
    shape = (STEPS, ROWS, D)
    quiet = jax.random.randint(key_quiet, (STEPS, ROWS, 1), 0, 4) == 0
    row_scale = jnp.where(quiet, jnp.float32(0.05), jnp.float32(1.0))
    values = jax.random.normal(key_values, shape, jnp.float32)
    return jnp.clip(values * row_scale, -6.0, 6.0).astype(jnp.bfloat16)


def draw_attn_out_weight(key, part):
    key = jax.random.fold_in(key, 15)
    key_values, key_order = jax.random.split(key, 2)
    shape = (HQ * HD, D)
    order = jax.random.permutation(key_order, EXPERTS).astype(jnp.float32)
    levels = jnp.exp(-1.5 + 2.5 * (order + 0.5) / EXPERTS)
    column_level = jnp.repeat(levels, D // EXPERTS)
    values = jax.random.normal(key_values, shape, jnp.float32)
    scaled = values * (HQ * HD) ** (-0.5) * column_level[None, :]
    return jnp.clip(scaled, -0.125, 0.125).astype(jnp.bfloat16)


def block_scale(own_key, shape, shards, smallest, top_value):
    loudness = 1.0
    for axis_at, shards_of in shards:
        steps = jax.random.uniform(jax.random.fold_in(jax.random.fold_in(own_key, 6), axis_at), (shards_of,), jnp.float32, smallest / len(shards), top_value / len(shards))
        loudness = loudness * jnp.repeat(jnp.exp(steps), shape[axis_at] // shards_of).reshape((-1,) + (1,) * (len(shape) - 1 - axis_at))
    return loudness


def routed_block(own_key, own, number, rows, amount, top, limit, skew):
    order = jax.random.permutation(own_key, amount)
    crowded, ordinary = shares(amount, rows * top, limit, skew, True), shares(amount, rows * top, limit, skew, False)
    places = jnp.arange(amount)

    def named(sizes, offset_by):
        used = int((sizes > 0).sum())
        fixed = max(1, used // 4)
        shifted = fixed + (places - fixed + offset_by * (used - fixed)) % max(1, amount - fixed)
        return jnp.zeros((amount,), jnp.int32).at[order[jnp.where(places < fixed, places, shifted)]].set(jnp.asarray(sizes, jnp.int32))

    sizes = jnp.where(number % 4 == 0, named(crowded, number // 4), named(ordinary, number - number // 4 - 1))
    mixed = jax.random.permutation(jax.random.fold_in(own, 3), amount)
    source_of, receiver = mixed[0:amount // 2 * 2:2], mixed[1:amount // 2 * 2:2]
    room = jnp.minimum(sizes[source_of] - 1, limit - sizes[receiver]) // 2
    room = jnp.where((source_of == order[0]) | (receiver == order[0]) | (sizes[receiver] == 0), 0, jnp.maximum(room, 0))
    shifted = jax.random.randint(jax.random.fold_in(own, 4), (amount // 2,), 0, 1 << 20) % (room + 1)
    sizes = sizes.at[source_of].add(-shifted).at[receiver].add(shifted)
    labels = jnp.searchsorted(jnp.cumsum(sizes), jnp.arange(rows * top), side="right").astype(jnp.int32)
    table = labels.reshape(top, rows).T
    table = table[jax.random.permutation(jax.random.fold_in(own, 1), rows)]
    offset_by = jax.random.randint(jax.random.fold_in(own, 2), (rows, 1), 0, top)
    return jnp.take_along_axis(table, (jnp.arange(top)[None, :] + offset_by) % top, axis=1)


def shares(number_of, total, reach, skew, full):
    loads = [(1 << 20) // math.isqrt(rank ** skew) + 1 for rank in range(1, number_of + 1)]
    largest = reach if full else min(reach, max(-(-total // number_of), total * loads[0] // sum(loads)))
    least = 1 if total - largest >= number_of - 1 else 0
    given, rest = [largest] + [least] * (number_of - 1), total - largest - least * (number_of - 1)
    while rest > 0:
        candidates = [i for i in range(1, number_of) if given[i] < largest] or [i for i in range(1, number_of) if given[i] < reach]
        pool, left = sum([loads[i] for i in candidates]), rest
        for i in candidates:
            extra = min(reach - given[i], max(1, left * loads[i] // pool), rest)
            given[i] = given[i] + extra
            rest = rest - extra
    return np.array(given)


def bell_draw(key, dims, spread, limit, cuts=(), kind=jnp.bfloat16):
    values = jax.random.normal(key, dims, jnp.float32) * spread
    if len(cuts) > 0:
        values = block_scale(key, dims, cuts, -0.22, 0.18) * values
    return jnp.clip(values, min=-limit, max=limit).astype(kind)


def setup_inputs(seed: int = 0) -> dict:
    keys = jax.random.split(jax.random.key(seed), 14)
    queries = draw_queries(jax.random.fold_in(keys[13], 71), 0)
    cache_keys = draw_cache_keys(jax.random.fold_in(keys[13], 71), 0)
    cache_values = bell_draw(keys[2], (ROWS, CACHE, KVH * HD), 1.0, 6.0, ((0, 128), (2, 2)))
    new_keys = bell_draw(keys[3], (STEPS, ROWS, KVH * HD), 1.0, 6.0, ((1, 128), (2, 2)))
    new_values = bell_draw(keys[4], (STEPS, ROWS, KVH * HD), 1.0, 6.0, ((1, 128), (2, 2)))
    lengths = draw_lengths(jax.random.fold_in(keys[13], 71), 0)
    attn_out_weight = draw_attn_out_weight(jax.random.fold_in(keys[13], 71), 0)
    residual = draw_residual(jax.random.fold_in(keys[13], 71), 0)
    norm_gain = jnp.clip(1.0 + 0.18 * jax.random.normal(keys[8], (D,), jnp.float32), 0.1, 1.9)
    expert_ids_keys = jax.random.split(jax.random.fold_in(keys[9], 1), STEPS * ROWS // BLOCK)
    expert_ids_turns = jax.random.permutation(jax.random.fold_in(keys[9], 3), STEPS * ROWS // BLOCK)
    expert_ids = jax.vmap(lambda own, number: routed_block(jax.random.fold_in(keys[9], 2), own, number, BLOCK, EXPERTS, TOPK, CAP, 2))(expert_ids_keys, expert_ids_turns).reshape((STEPS, ROWS, TOPK))
    gate_weights = jnp.clip(0.049804688 + 0.2998047 * jax.random.uniform(keys[10], (STEPS, ROWS, TOPK), jnp.float32) ** block_scale(keys[10], (STEPS, ROWS, TOPK), ((1, 8),), -0.2, 0.2), 0.049804688, 0.34960938).astype(jnp.bfloat16)
    expert_in = bell_draw(keys[11], (EXPERTS, D, 2, FF), D ** -0.5, 0.09375, ((0, 16), (1, 8), (3, 2)))
    expert_out = bell_draw(keys[12], (EXPERTS, FF, D), FF ** -0.5, 0.15625, ((0, 16), (1, 2), (2, 8)))
    return {"queries": queries, "cache_keys": cache_keys, "cache_values": cache_values, "new_keys": new_keys, "new_values": new_values, "lengths": lengths, "attn_out_weight": attn_out_weight, "residual": residual, "norm_gain": norm_gain, "expert_ids": expert_ids, "gate_weights": gate_weights, "expert_in": expert_in, "expert_out": expert_out}


norm_eps = 1e-06

def attend_group(group):
    queries, keys_cache, values_cache, keys_fresh, values_fresh, seq_lengths = group
    step_count = queries.shape[0]
    row_count = queries.shape[1]
    group_size = HQ // KVH
    query_heads = queries.astype(jnp.float32).reshape(step_count, row_count, KVH, group_size, HD)
    cache_heads = keys_cache.astype(jnp.float32).reshape(row_count, CACHE, KVH, HD)
    value_heads = values_cache.astype(jnp.float32).reshape(row_count, CACHE, KVH, HD)
    fresh_keys = keys_fresh.astype(jnp.float32).reshape(step_count, row_count, KVH, HD)
    fresh_values = values_fresh.astype(jnp.float32).reshape(step_count, row_count, KVH, HD)
    score_scale = HD ** (-0.5)
    cache_scores = jnp.einsum('srkgd,rpkd->srkgp', query_heads, cache_heads) * score_scale
    live_cache = jnp.arange(CACHE, dtype=jnp.int32)[None, :] < seq_lengths[:, None]
    cache_scores = jnp.where(live_cache[None, :, None, None, :], cache_scores, -jnp.inf)
    fresh_scores = jnp.einsum('srkgd,jrkd->srkgj', query_heads, fresh_keys) * score_scale
    step_index = jnp.arange(step_count, dtype=jnp.int32)
    causal = step_index[None, :] <= step_index[:, None]
    fresh_scores = jnp.where(causal[:, None, None, None, :], fresh_scores, -jnp.inf)
    row_max = jnp.maximum(lax.optimization_barrier(jnp.max(cache_scores, axis=-1)), lax.optimization_barrier(jnp.max(fresh_scores, axis=-1)))[..., None]
    cache_exp = jnp.exp(cache_scores - row_max)
    fresh_exp = jnp.exp(fresh_scores - row_max)
    row_total = lax.optimization_barrier(jnp.sum(cache_exp, axis=-1, keepdims=True)) + lax.optimization_barrier(jnp.sum(fresh_exp, axis=-1, keepdims=True))
    cache_probs = lax.optimization_barrier((cache_exp / row_total).astype(jnp.bfloat16)).astype(jnp.float32)
    fresh_probs = lax.optimization_barrier((fresh_exp / row_total).astype(jnp.bfloat16)).astype(jnp.float32)
    combined = jnp.einsum('srkgp,rpkd->srkgd', cache_probs, value_heads)
    combined = combined + jnp.einsum('srkgj,jrkd->srkgd', fresh_probs, fresh_values)
    return combined.astype(jnp.bfloat16).reshape(step_count, row_count, HQ * HD)

def reference(queries, cache_keys, cache_values, new_keys, new_values, lengths, attn_out_weight, residual, norm_gain, expert_ids, gate_weights, expert_in, expert_out):
    group_count = ROWS // ROW_DEV

    def steps_first(array):
        width = array.shape[2]
        return jnp.transpose(array.reshape(STEPS, group_count, ROW_DEV, width), (1, 0, 2, 3))

    def rows_first(array):
        return array.reshape(group_count, ROW_DEV, array.shape[1], array.shape[2])
    grouped = (steps_first(queries), rows_first(cache_keys), rows_first(cache_values), steps_first(new_keys), steps_first(new_values), lengths.reshape(group_count, ROW_DEV))
    attn = lax.map(attend_group, grouped)
    attn = jnp.transpose(attn, (1, 0, 2, 3)).reshape(STEPS * ROWS, HQ * HD)
    projected = jnp.dot(attn, attn_out_weight, preferred_element_type=jnp.float32).reshape(STEPS, ROWS, D)
    attended = residual.astype(jnp.float32) + projected
    mean_square = lax.optimization_barrier(jnp.mean(attended * attended, axis=-1, keepdims=True))
    normed = (attended * lax.rsqrt(mean_square + norm_eps) * norm_gain).astype(jnp.bfloat16)
    replicas = ROWS // BLOCK
    normed_blocks = normed.reshape(STEPS, replicas, BLOCK, D).astype(jnp.float32)
    route_ids = expert_ids.reshape(STEPS, replicas, BLOCK, TOPK)
    route_gates = gate_weights.reshape(STEPS, replicas, BLOCK, TOPK).astype(jnp.float32)
    expert_range = jnp.arange(EXPERTS, dtype=jnp.int32)
    chosen = route_ids[..., None] == expert_range
    onehot = lax.optimization_barrier(jnp.sum(chosen.astype(jnp.int32), axis=3))
    slot_rank = jnp.cumsum(onehot, axis=2) - 1
    gate_pick = lax.optimization_barrier(jnp.sum(jnp.where(chosen, route_gates[..., None], jnp.float32(0.0)), axis=3))
    slot_range = jnp.arange(CAP, dtype=jnp.int32)

    def one_expert(running, inputs):
        expert_index, weight_in, weight_out = inputs
        hit_rows = lax.dynamic_index_in_dim(onehot, expert_index, 3, keepdims=False)
        rank_rows = lax.dynamic_index_in_dim(slot_rank, expert_index, 3, keepdims=False)
        gate_rows = lax.dynamic_index_in_dim(gate_pick, expert_index, 3, keepdims=False)
        select = ((rank_rows[:, :, None, :] == slot_range[None, None, :, None]) & (hit_rows[:, :, None, :] > 0)).astype(jnp.float32)
        expert_rows = jnp.einsum('srcb,srbd->srcd', select, normed_blocks).astype(jnp.bfloat16).reshape(-1, D)
        gate_up = jnp.dot(expert_rows, weight_in.reshape(D, 2 * FF), preferred_element_type=jnp.float32)
        hidden = (jax.nn.silu(gate_up[:, :FF]) * gate_up[:, FF:]).astype(jnp.bfloat16)
        result = jnp.dot(hidden, weight_out, preferred_element_type=jnp.float32).astype(jnp.bfloat16)
        result = result.reshape(STEPS, replicas, CAP, D).astype(jnp.float32)
        weighted = select * gate_rows[:, :, None, :]
        return (running + jnp.einsum('srcb,srcd->srbd', weighted, result), None)
    start_sum = jnp.zeros((STEPS, replicas, BLOCK, D), jnp.float32)
    routed, _ = lax.scan(one_expert, start_sum, (expert_range, expert_in, expert_out))
    return (attended + routed.reshape(STEPS, ROWS, D)).astype(jnp.bfloat16)
```

```python
import jax
import jax.numpy as jnp
from jax import lax
from jax.sharding import PartitionSpec as P

D = 4096
HD = 128


norm_eps = 1e-06


def attend_rows(queries, cache_keys, cache_values, new_keys, new_values, lengths):
    step_count, row_count, query_width = queries.shape
    cache_len = cache_keys.shape[1]
    kv_heads = cache_keys.shape[2] // HD
    group_size = query_width // (kv_heads * HD)
    query_heads = queries.reshape(step_count, row_count, kv_heads, group_size, HD)
    cache_heads = cache_keys.reshape(row_count, cache_len, kv_heads, HD)
    value_heads = cache_values.reshape(row_count, cache_len, kv_heads, HD)
    fresh_keys = new_keys.reshape(step_count, row_count, kv_heads, HD)
    fresh_values = new_values.reshape(step_count, row_count, kv_heads, HD)
    score_scale = HD ** (-0.5)
    cache_scores = (
        jnp.einsum(
            "srkgd,rpkd->srkgp", query_heads, cache_heads, preferred_element_type=jnp.float32
        )
        * score_scale
    )
    live_cache = jnp.arange(cache_len, dtype=jnp.int32)[None, :] < lengths[:, None]
    cache_scores = jnp.where(live_cache[None, :, None, None, :], cache_scores, -jnp.inf)
    fresh_scores = (
        jnp.einsum("srkgd,jrkd->srkgj", query_heads, fresh_keys, preferred_element_type=jnp.float32)
        * score_scale
    )
    step_index = jnp.arange(step_count, dtype=jnp.int32)
    causal = step_index[None, :] <= step_index[:, None]
    fresh_scores = jnp.where(causal[:, None, None, None, :], fresh_scores, -jnp.inf)
    row_max = jnp.maximum(jnp.max(cache_scores, axis=-1), jnp.max(fresh_scores, axis=-1))[..., None]
    cache_exp = jnp.exp(cache_scores - row_max)
    fresh_exp = jnp.exp(fresh_scores - row_max)
    row_total = jnp.sum(cache_exp, axis=-1, keepdims=True) + jnp.sum(
        fresh_exp, axis=-1, keepdims=True
    )
    cache_probs = (cache_exp / row_total).astype(jnp.bfloat16)
    fresh_probs = (fresh_exp / row_total).astype(jnp.bfloat16)
    combined = jnp.einsum(
        "srkgp,rpkd->srkgd", cache_probs, value_heads, preferred_element_type=jnp.float32
    )
    combined = combined + jnp.einsum(
        "srkgj,jrkd->srkgd", fresh_probs, fresh_values, preferred_element_type=jnp.float32
    )
    return combined.astype(jnp.bfloat16).reshape(step_count, row_count, query_width)


ZH, Y, X = 4, 4, 4
bf16 = jnp.bfloat16
f32 = jnp.float32


def across_chip():
    return [(r, r ^ 1) for r in range(2 * ZH)]


def along_z(d):
    return [(r, ((r // 2 + d) % ZH) * 2 + r % 2) for r in range(2 * ZH)]


def along_y(d):
    return [(f, ((f // X + d) % Y) * X + f % X) for f in range(Y * X)]


def along_x(d):
    return [(f, (f // X) * X + (f % X + d) % X) for f in range(Y * X)]


def swap_zy(other_half):
    pairs = []
    for z in range(ZH):
        for c in range(2):
            for y in range(Y):
                for x in range(X):
                    for t in range(2):
                        source = (((z * 2 + c) * Y + y) * X + x) * 2 + t
                        goal = (((y * 2 + c) * Y + z) * X + (x ^ (2 * c))) * 2 + (t ^ other_half)
                        pairs.append((source, goal))
    return pairs


ALL = ("rep", "fsdp", "tp")


def pieces_along(value, table):
    return jnp.stack([value] + [lax.ppermute(value, "fsdp", table(-d)) for d in range(1, 4)])


def unroll_first(value, shift):
    twice = jnp.concatenate([value, value], axis=0)
    return lax.dynamic_slice_in_dim(twice, value.shape[0] - shift, value.shape[0], axis=0)


def on_device(
    queries,
    cache_keys,
    cache_values,
    new_keys,
    new_values,
    lengths,
    attn_out_weight,
    residual,
    norm_gain,
    expert_ids,
    gate_weights,
    expert_in,
    expert_out,
):
    rep, fsdp = lax.axis_index("rep"), lax.axis_index("fsdp")
    z, c = rep // 2, rep % 2
    y, x = fsdp // X, fsdp % X
    steps, block, top = expert_ids.shape
    experts = Y * X
    cap = 48

    weight_pieces = [attn_out_weight] + [
        lax.ppermute(attn_out_weight, "rep", along_z(-d)) for d in range(1, ZH)
    ]
    mine = jnp.stack(weight_pieces)
    theirs = lax.ppermute(mine, "rep", across_chip())
    both = jnp.stack([jnp.where(c == 0, mine, theirs), jnp.where(c == 0, theirs, mine)], axis=1)
    out_rows = unroll_first(both, z).reshape(2 * ZH * attn_out_weight.shape[0], -1)

    near_in = expert_in[0].reshape(expert_in.shape[1], -1)
    far_in = lax.ppermute(near_in, "rep", across_chip())
    weight_out = lax.all_gather(expert_out[0], "rep", axis=0, tiled=False)

    swap_same, swap_cross = swap_zy(0), swap_zy(1)
    ids_there = lax.ppermute(expert_ids, ALL, swap_same)
    residual_there = lax.ppermute(residual, ALL, swap_same)
    gain_there = lax.ppermute(norm_gain, ALL, swap_same)

    slot_range = jnp.arange(cap, dtype=jnp.int32)

    def routing(ids):
        chosen = ids[..., None] == jnp.arange(experts, dtype=jnp.int32)
        onehot = jnp.sum(chosen.astype(jnp.int32), axis=2)
        rank = jnp.cumsum(onehot, axis=1) - 1
        rank = jnp.transpose(rank, (0, 2, 1))
        hit = jnp.transpose(onehot, (0, 2, 1)) > 0
        selector = (rank[:, :, None, :] == slot_range[None, None, :, None]) & hit[:, :, None, :]
        return chosen, selector.astype(bf16)

    _, selector_there = routing(ids_there)
    chosen, selector = routing(expert_ids)
    gate_pick = jnp.sum(
        jnp.where(chosen, gate_weights.astype(f32)[..., None], f32(0.0)), axis=2
    ).astype(bf16)
    combiner = selector * jnp.transpose(gate_pick, (0, 2, 1))[:, :, None, :]

    attn = attend_rows(queries, cache_keys, cache_values, new_keys, new_values, lengths)
    seqs, width = attn.shape[1], attn.shape[2]
    rows = attn.reshape(steps * seqs, width)
    first, second = rows[:, : width // 2], rows[:, width // 2 :]
    first = pieces_along(pieces_along(first, along_x), along_y)
    second = pieces_along(pieces_along(second, along_y), along_x)
    model = out_rows.shape[1]
    partial = jnp.dot(
        first.reshape(-1, width // 2), out_rows[: width // 2], preferred_element_type=f32
    ).reshape(Y, X, steps * seqs, model)
    partial = partial + jnp.swapaxes(
        jnp.dot(
            second.reshape(-1, width // 2), out_rows[width // 2 :], preferred_element_type=f32
        ).reshape(X, Y, steps * seqs, model),
        0,
        1,
    )
    partial = partial.astype(bf16)
    partial = unroll_first(partial, y)
    partial = jnp.swapaxes(unroll_first(jnp.swapaxes(partial, 0, 1), x), 0, 1)
    partial = jnp.transpose(
        partial.reshape(Y * X, steps, seqs, model), (1, 0, 2, 3)
    ).reshape(steps, block, model)

    there_same = lax.ppermute(partial, ALL, swap_same)
    there_cross = lax.ppermute(partial, ALL, swap_cross)
    here_cross = lax.ppermute(partial, "tp", [(0, 1), (1, 0)])

    attended_there = residual_there.astype(f32) + (
        there_same.astype(f32) + there_cross.astype(f32)
    )
    scaled = (attended_there * gain_there).astype(bf16)
    dispatched = jnp.einsum(
        "secb,sbd->escd", selector_there, scaled, preferred_element_type=f32
    ).astype(bf16)
    arrived = lax.all_to_all(
        dispatched.reshape(experts, steps * cap, model), "fsdp", split_axis=0, concat_axis=0, tiled=True
    ).reshape(ZH, 2, 2, steps * cap, model)

    attended = residual.astype(f32) + (partial.astype(f32) + here_cross.astype(f32))
    squares = jnp.sum(attended * attended, axis=-1)
    squares = jnp.sum(pieces_along(squares, along_x), axis=0)
    squares = jnp.sum(pieces_along(squares, along_y), axis=0)
    row_scale = lax.rsqrt(squares / D + norm_eps)
    own_selector = lax.dynamic_index_in_dim(selector, fsdp, axis=1, keepdims=False)
    slot_scale = jnp.sum(own_selector.astype(f32) * row_scale[:, None, :], axis=-1).reshape(
        steps * cap, 1
    )

    near_w = near_in.reshape(2, model, -1)
    far_w = far_in.reshape(2, model, -1)

    def gate_up_of(d):
        part = lax.dynamic_index_in_dim(arrived, (z + d) % ZH, axis=0, keepdims=False)
        total = sum(
            jnp.dot(part[i, j], w[j], preferred_element_type=f32)
            for i, w in enumerate((near_w, far_w))
            for j in range(2)
        )
        return total

    received = [
        lax.ppermute(gate_up_of(d).astype(bf16), "rep", along_z(d)) for d in range(1, ZH)
    ]
    gate_up = gate_up_of(0)
    for part in received:
        gate_up = gate_up + part.astype(f32)
    gate_up = gate_up * slot_scale
    half = gate_up.shape[1] // 2
    hidden = (jax.nn.silu(gate_up[:, :half]) * gate_up[:, half:]).astype(bf16)
    result = jnp.einsum("sh,rhd->rsd", hidden, weight_out, preferred_element_type=f32).astype(bf16)
    result = jnp.swapaxes(result.reshape(2 * ZH, steps * cap, 2, model), 1, 2)
    returned = lax.all_to_all(
        result.reshape(experts, steps * cap, model), "fsdp", split_axis=0, concat_axis=0, tiled=True
    ).reshape(experts, steps, cap, model)
    routed = jnp.einsum("secb,escd->sbd", combiner, returned, preferred_element_type=f32).astype(bf16)
    routed_cross = lax.ppermute(routed, "tp", [(0, 1), (1, 0)])
    return (attended + (routed.astype(f32) + routed_cross.astype(f32))).astype(bf16)


def solution(mesh):
    placed = (
        P(None, ("rep", "fsdp"), "tp"),
        P(("rep", "fsdp"), None, "tp"),
        P(("rep", "fsdp"), None, "tp"),
        P(None, ("rep", "fsdp"), "tp"),
        P(None, ("rep", "fsdp"), "tp"),
        P(("rep", "fsdp")),
        P(("tp", "rep"), "fsdp"),
        P(None, "rep", "fsdp"),
        P("fsdp"),
        P(None, "rep", None),
        P(None, "rep", None),
        P("fsdp", "rep", None, "tp"),
        P("fsdp", "tp", "rep"),
    )
    return jax.shard_map(
        on_device, mesh=mesh, in_specs=placed, out_specs=P(None, "rep", "fsdp"), check_vma=False
    )
```

```python
import functools

import jax
import jax.numpy as jnp
from jax import lax
from jax.experimental import pallas as pl
from jax.experimental.pallas import tpu as pltpu
from jax.sharding import PartitionSpec as P

D = 4096
HD = 128
ZH, Y, X = 4, 4, 4
CAP = 48
PLACES = ("rep", "fsdp")
OTHER_HALF = [(0, 1), (1, 0)]
norm_eps = 1e-06
bf16 = jnp.bfloat16
f32 = jnp.float32
i32 = jnp.int32
NT = (((1,), (1,)), ((), ()))
VMEM = pl.BlockSpec(memory_space=pltpu.VMEM)
ANY = pl.BlockSpec(memory_space=pl.ANY)
SMEM = pl.BlockSpec(memory_space=pltpu.SMEM)
ROOM = pltpu.CompilerParams(vmem_limit_bytes=48 * 1024 * 1024)


def across_chip():
    return [(r, r ^ 1) for r in range(2 * ZH)]


def along_z(d):
    return [(r, ((r // 2 + d) % ZH) * 2 + r % 2) for r in range(2 * ZH)]


def swap_zy():
    pairs = []
    for z in range(ZH):
        for c in range(2):
            for y in range(Y):
                for x in range(X):
                    goal = ((y * 2 + c) * Y + z) * X + (x ^ (2 * c))
                    pairs.append((((z * 2 + c) * Y + y) * X + x, goal))
    return pairs


def cost(us):
    return pl.CostEstimate(flops=0, bytes_accessed=us * 3600000, transcendentals=0)


def iota(shape, axis):
    return lax.broadcasted_iota(i32, shape, axis)


def attention_kernel(
    lengths, q, keys, values, nk, nv, out, q_wide, q_rows, fresh, o_rows, ck, cv, arrival
):
    steps, seqs, width = q.shape
    cached = ck.shape[1]
    kv_heads = ck.shape[2] // HD
    group = width // (kv_heads * HD)
    rows = group * steps
    scale = HD ** (-0.5)
    copies = [
        [
            pltpu.make_async_copy(whole.at[b], held.at[b], arrival.at[i, b])
            for i, (whole, held) in enumerate(((keys, ck), (values, cv)))
        ]
        for b in range(seqs)
    ]
    for pair in copies:
        for copy in pair:
            copy.start()
    q_wide[...] = q[...].astype(f32)
    fresh[...] = jnp.zeros_like(fresh)
    place = iota((rows, cached), 1)
    fresh_place = iota((rows, HD), 1)
    live_fresh = fresh_place <= iota((rows, HD), 0) % steps
    for b in range(seqs):
        live = place < lengths[b]
        for copy in copies[b]:
            copy.wait()
        for k in range(kv_heads):
            lanes = pl.ds(k * HD, HD)
            for g in range(group):
                q_rows[pl.ds(g * steps, steps), :] = q_wide[
                    :, b, pl.ds((k * group + g) * HD, HD)
                ]
            for j in range(steps):
                fresh[0, pl.ds(j, 1), :] = nk[j, pl.ds(b, 1), lanes].astype(f32)
                fresh[1, pl.ds(j, 1), :] = nv[j, pl.ds(b, 1), lanes].astype(f32)
            rows_q = q_rows[...].astype(bf16)
            old = lax.dot_general(rows_q, ck[b, :, lanes], NT, preferred_element_type=f32) * scale
            new = (
                lax.dot_general(rows_q, fresh[0].astype(bf16), NT, preferred_element_type=f32) * scale
            )
            old = jnp.where(live, old, -jnp.inf)
            new = jnp.where(live_fresh, new, -jnp.inf)
            top = jnp.maximum(
                jnp.max(old, axis=1, keepdims=True), jnp.max(new, axis=1, keepdims=True)
            )
            old = jnp.exp(old - top)
            new = jnp.exp(new - top)
            share = 1.0 / (
                jnp.sum(old, axis=1, keepdims=True) + jnp.sum(new, axis=1, keepdims=True)
            )
            mixed = jnp.dot(
                (old * share).astype(bf16), cv[b, :, lanes], preferred_element_type=f32
            ) + jnp.dot(
                (new * share).astype(bf16), fresh[1].astype(bf16), preferred_element_type=f32
            )
            for g in range(group):
                o_rows[pl.ds(b * steps, steps), pl.ds((k * group + g) * HD, HD)] = mixed[
                    g * steps : (g + 1) * steps, :
                ]
    done = o_rows[...].astype(bf16)
    for f in range(out.shape[0]):
        out[f] = done


def attention(lengths, q, ck, cv, nk, nv, copies):
    steps, seqs, width = q.shape
    rows = steps * seqs
    group = width // ck.shape[2]
    return pl.pallas_call(
        attention_kernel,
        out_shape=jax.ShapeDtypeStruct((copies, rows, width), bf16),
        in_specs=[SMEM, VMEM, ANY, ANY, VMEM, VMEM],
        out_specs=VMEM,
        scratch_shapes=[
            pltpu.VMEM((steps, seqs, width), f32),
            pltpu.VMEM((group * steps, HD), f32),
            pltpu.VMEM((2, HD, HD), f32),
            pltpu.VMEM((rows, width), f32),
            pltpu.VMEM(ck.shape, bf16),
            pltpu.VMEM(cv.shape, bf16),
            pltpu.SemaphoreType.DMA((2, seqs)),
        ],
        compiler_params=ROOM,
        cost_estimate=cost(7),
        name="attention",
    )(lengths, q, ck, cv, nk, nv)


def project_kernel(place, attn, mine, theirs, out):
    rows, width = out.shape
    steps = 4
    depth = mine.shape[1]
    total = jnp.zeros((rows, width), f32)
    for d in range(ZH):
        for same, held in ((True, mine), (False, theirs)):
            z = lax.rem(place[0] + ZH - d, ZH)
            r = 2 * z + (place[1] if same else 1 - place[1])
            columns = pl.ds(pl.multiple_of(r * depth, depth), depth)
            total = total + jnp.dot(attn[:, columns], held[d], preferred_element_type=f32)
    by_step = jnp.swapaxes(total.reshape(rows // steps, steps, width), 0, 1)
    out[...] = by_step.reshape(rows, width).astype(bf16)


def project(place, attn, mine, theirs):
    return pl.pallas_call(
        project_kernel,
        out_shape=jax.ShapeDtypeStruct((attn.shape[0], mine.shape[2]), bf16),
        in_specs=[SMEM] + [VMEM] * 3,
        out_specs=VMEM,
        compiler_params=ROOM,
        cost_estimate=cost(3),
        name="project",
    )(place, attn, mine, theirs)


def dispatch_kernel(ids, scaled, out):
    experts, slots, _ = out.shape
    top, rows = ids.shape
    block = rows // (slots // CAP)
    expert = iota((experts, rows), 0)
    hit = jnp.zeros((experts, rows), jnp.bool_)
    for k in range(top):
        hit = hit | (ids[pl.ds(k, 1), :] == expert)
    before, after = iota((rows, rows), 0), iota((rows, rows), 1)
    earlier = (before <= after) & (before // block == after // block)
    rank = jnp.dot(
        hit.astype(f32).astype(bf16), earlier.astype(f32).astype(bf16), preferred_element_type=f32
    ).astype(i32)
    slot_of = jnp.where(hit, iota((experts, rows), 1) // block * CAP + rank - 1, -1)
    slot = iota((slots, rows), 0)
    for e in range(experts):
        pick = jnp.where(slot_of[e : e + 1, :] == slot, f32(1.0), f32(0.0)).astype(bf16)
        out[e] = jnp.dot(pick, scaled[...], preferred_element_type=f32).astype(bf16)


def dispatch(ids, scaled, experts, steps):
    return pl.pallas_call(
        dispatch_kernel,
        out_shape=jax.ShapeDtypeStruct((experts, steps * CAP, scaled.shape[1]), bf16),
        in_specs=[VMEM] * 2,
        out_specs=VMEM,
        compiler_params=ROOM,
        cost_estimate=cost(2),
        name="dispatch",
    )(ids, scaled)


def expand_rows(place, arrived, near, far, ahead):
    total = None
    for i in range(4):
        held = (near, far)[i // 2][i % 2]
        rows = jnp.concatenate([arrived[4 * lax.rem(place[0] + d, ZH) + i] for d in ahead])
        part = jnp.dot(rows, held, preferred_element_type=f32)
        total = part if total is None else total + part
    return total


def expand_far_kernel(place, arrived, near, far, low, high):
    total = expand_rows(place, arrived, near, far, (2,))
    half = total.shape[0] // 2
    low[...] = total[:half].astype(bf16)
    high[...] = total[half:].astype(bf16)


def expand_near_kernel(place, arrived, near, far, plus, minus, own):
    total = expand_rows(place, arrived, near, far, (1, 3, 0))
    slots = own.shape[0]
    for i, out in enumerate((plus, minus, own)):
        out[...] = total[i * slots : (i + 1) * slots]


def expand_far(place, arrived, near, far):
    half, width = arrived.shape[1] // 2, near.shape[2]
    return pl.pallas_call(
        expand_far_kernel,
        out_shape=[jax.ShapeDtypeStruct((half, width), bf16)] * 2,
        in_specs=[SMEM] + [VMEM] * 3,
        out_specs=[VMEM] * 2,
        compiler_params=ROOM,
        cost_estimate=cost(2),
        name="expand_far",
    )(place, arrived, near, far)


def expand_near(place, arrived, near, far):
    slots, width = arrived.shape[1], near.shape[2]
    return pl.pallas_call(
        expand_near_kernel,
        out_shape=[jax.ShapeDtypeStruct((slots, width), f32)] * 3,
        in_specs=[SMEM] + [VMEM] * 3,
        out_specs=[VMEM] * 3,
        compiler_params=ROOM,
        cost_estimate=cost(4),
        name="expand_near",
    )(place, arrived, near, far)


def contract_kernel(steps, place, ids, squares, own, one, two, *refs):
    *weights, out = refs
    slots, width = out.shape[1:]
    half = own.shape[1] // 2
    top, rows = ids.shape
    block = rows // steps
    total = jnp.sum(squares[...], axis=0, keepdims=True)
    row_scale = lax.rsqrt(total / D + norm_eps)
    hit = jnp.zeros((8, rows), jnp.bool_)
    for k in range(top):
        hit = hit | (jnp.broadcast_to(ids[pl.ds(k, 1), :], (8, rows)) == place[2])
    before, after = iota((rows, rows), 0), iota((rows, rows), 1)
    earlier = (before <= after) & (before // block == after // block)
    rank = jnp.dot(
        hit.astype(f32).astype(bf16), earlier.astype(f32).astype(bf16), preferred_element_type=f32
    ).astype(i32)
    slot_of = jnp.where(hit, iota((8, rows), 1) // block * CAP + rank - 1, -1)
    pick = slot_of[0:1, :] == iota((slots, rows), 0)
    slot_scale = jnp.sum(jnp.where(pick, row_scale, 0.0), axis=1, keepdims=True)
    both = (own[...] + (one[...].astype(f32) + two[...].astype(f32))) * slot_scale
    gate, up = both[:, :half], both[:, half:]
    hidden = (gate / (1.0 + jnp.exp(-gate)) * up).astype(bf16)
    split = half // 2
    for r in range(weights[0].shape[0]):
        result = jnp.dot(hidden[:, :split], weights[0][r], preferred_element_type=f32)
        result = result + jnp.dot(hidden[:, split:], weights[1][r], preferred_element_type=f32)
        for i in range(2):
            out[2 * r + i] = result[:, i * width : (i + 1) * width].astype(bf16)


def contract(steps, place, ids, squares, parts, weights, experts, width):
    slots = parts[0].shape[0]
    return pl.pallas_call(
        functools.partial(contract_kernel, steps),
        out_shape=jax.ShapeDtypeStruct((experts, slots, width), bf16),
        in_specs=[SMEM] + [VMEM] * (2 + len(parts) + len(weights)),
        out_specs=VMEM,
        compiler_params=ROOM,
        cost_estimate=cost(5),
        name="contract",
    )(place, ids, squares, *parts, *weights)


def combine_kernel(steps, ids, gates, *refs):
    *returned, out = refs
    experts, slots, _ = returned[0].shape
    rows, top = ids.shape
    block = rows // steps
    expert = iota((rows, experts), 1)
    hit = jnp.zeros((rows, experts), jnp.bool_)
    gate = jnp.zeros((rows, experts), f32)
    wide_gates = gates[...].astype(f32)
    for k in range(top):
        named = ids[:, k : k + 1] == expert
        hit = hit | named
        gate = jnp.where(named, wide_gates[:, k : k + 1], gate)
    after, before = iota((rows, rows), 0), iota((rows, rows), 1)
    earlier = (before <= after) & (before // block == after // block)
    rank = jnp.dot(
        earlier.astype(f32).astype(bf16), hit.astype(f32).astype(bf16), preferred_element_type=f32
    ).astype(i32)
    slot_of = jnp.where(hit, iota((rows, experts), 0) // block * CAP + rank - 1, -1)
    part = rows // len(returned)
    for i, held in enumerate(returned):
        slot = iota((part, slots), 1) + i * slots
        total = jnp.zeros((part, out.shape[1]), f32)
        of, by = slot_of[i * part : (i + 1) * part], gate[i * part : (i + 1) * part]
        for e in range(experts):
            weights = jnp.where(of[:, e : e + 1] == slot, by[:, e : e + 1], 0.0).astype(bf16)
            total = total + jnp.dot(weights, held[e], preferred_element_type=f32)
        out[pl.ds(i * part, part), :] = total.astype(bf16)


def combine(steps, ids, gates, returned):
    return pl.pallas_call(
        functools.partial(combine_kernel, steps),
        out_shape=jax.ShapeDtypeStruct((ids.shape[0], returned[0].shape[2]), bf16),
        in_specs=[VMEM] * (2 + len(returned)),
        out_specs=VMEM,
        compiler_params=ROOM,
        cost_estimate=cost(2),
        name="combine",
    )(ids, gates, *returned)


def on_device(
    queries,
    cache_keys,
    cache_values,
    new_keys,
    new_values,
    lengths,
    attn_out_weight,
    residual,
    norm_gain,
    expert_ids,
    gate_weights,
    expert_in,
    expert_out,
):
    rep, fsdp = lax.axis_index("rep"), lax.axis_index("fsdp")
    z, c = rep // 2, rep % 2
    place = jnp.stack([z, c, fsdp, lax.axis_index("tp")]).astype(i32)
    steps, block, top = expert_ids.shape
    experts = Y * X
    rows, model = steps * block, residual.shape[2]
    ids_by_step = expert_ids.reshape(rows, top)
    ids_across = jnp.transpose(ids_by_step)

    def shift(value, d):
        return lax.ppermute(value, "rep", along_z(d))

    def core(value):
        return lax.ppermute(value, "rep", across_chip())

    proj_minus, proj_plus = shift(attn_out_weight, 1), shift(attn_out_weight, -1)
    ids_there = lax.ppermute(ids_across, PLACES, swap_zy())
    attn = attention(lengths, queries, cache_keys, cache_values, new_keys, new_values, experts)
    quarter = expert_out.shape[1] // 2
    out_first, out_second = expert_out[0, :quarter], expert_out[0, quarter:]
    attn, ids_there, proj_minus, proj_plus, out_first = lax.optimization_barrier(
        (attn, ids_there, proj_minus, proj_plus, out_first)
    )
    out_first = lax.all_gather(out_first, "rep", axis=0, tiled=False)
    split = proj_minus.shape[0] // 2
    proj_far = [shift(proj_minus[:split], 1), shift(proj_plus[split:], -1)]

    near_in = expert_in[0].reshape(expert_in.shape[1], -1)
    attn, near_in = lax.optimization_barrier((attn, near_in))
    far_in = core(near_in)
    attn = lax.all_to_all(attn, "fsdp", split_axis=0, concat_axis=0, tiled=True)
    mine = jnp.stack([attn_out_weight, proj_minus, jnp.concatenate(proj_far), proj_plus])
    attn, mine, theirs = lax.optimization_barrier((attn, mine, core(mine)))
    near_in, far_in = near_in.reshape(2, model, -1), far_in.reshape(2, model, -1)
    partial = project(place, attn.reshape(rows, -1), mine, theirs)
    here_cross = lax.ppermute(partial, "tp", OTHER_HALF)
    attended = residual.astype(f32).reshape(rows, model) + (
        partial.astype(f32) + here_cross.astype(f32)
    )
    scaled = (attended * norm_gain).astype(bf16)
    there = lax.ppermute(scaled, PLACES, swap_zy())

    there, out_second = lax.optimization_barrier((there, out_second))
    out_second = lax.all_gather(out_second, "rep", axis=0, tiled=False)
    dispatched = dispatch(ids_there, there, experts, steps)
    arrived = lax.all_to_all(dispatched, "fsdp", split_axis=0, concat_axis=0, tiled=True)

    low, high = expand_far(place, arrived, near_in, far_in)
    low, high = shift(low, 1), shift(high, -1)
    plus, minus, own = expand_near(place, arrived, near_in, far_in)
    half = low.shape[0]
    low, high, plus, minus = lax.optimization_barrier((low, high, plus, minus))
    plus = jnp.concatenate([plus[:half] + low.astype(f32), plus[half:]]).astype(bf16)
    minus = jnp.concatenate([minus[:half], minus[half:] + high.astype(f32)]).astype(bf16)
    squares = jnp.sum(attended * attended, axis=-1).reshape(steps, block)
    squares, plus, minus = lax.optimization_barrier((squares, plus, minus))
    plus, minus = shift(plus, 1), shift(minus, -1)
    squares = lax.all_gather(squares, "fsdp", axis=0, tiled=False).reshape(experts, rows)

    result = contract(
        steps,
        place,
        ids_across,
        squares,
        [own, plus, minus],
        [out_first, out_second],
        experts,
        model,
    )
    returned = lax.all_to_all(result, "fsdp", split_axis=0, concat_axis=0, tiled=True)
    routed = combine(steps, ids_by_step, gate_weights.reshape(rows, top), [returned])
    routed_cross = lax.ppermute(routed, "tp", OTHER_HALF)
    routed = routed.astype(f32) + routed_cross.astype(f32)
    return (attended + routed).astype(bf16).reshape(steps, block, model)


def solution(mesh):
    placed = (
        P(None, ("rep", "fsdp"), "tp"),
        P(("rep", "fsdp"), None, "tp"),
        P(("rep", "fsdp"), None, "tp"),
        P(None, ("rep", "fsdp"), "tp"),
        P(None, ("rep", "fsdp"), "tp"),
        P(("rep", "fsdp")),
        P(("tp", "rep"), "fsdp"),
        P(None, "rep", "fsdp"),
        P("fsdp"),
        P(None, "rep", None),
        P(None, "rep", None),
        P("fsdp", "rep", None, "tp"),
        P("fsdp", "tp", "rep"),
    )
    return jax.shard_map(
        on_device, mesh=mesh, in_specs=placed, out_specs=P(None, "rep", "fsdp"), check_vma=False
    )
```

```python
import functools

import jax
import jax.numpy as jnp
from jax import lax
from jax.experimental import pallas as pl
from jax.experimental.pallas import tpu as pltpu
from jax.sharding import PartitionSpec as P

D = 4096
HD = 128
ZH, Y, X = 4, 4, 4
CAP = 48
PLACES = ("rep", "fsdp")
OTHER_HALF = [(0, 1), (1, 0)]
norm_eps = 1e-06
bf16 = jnp.bfloat16
f32 = jnp.float32
i32 = jnp.int32
NT = (((1,), (1,)), ((), ()))
VMEM = pl.BlockSpec(memory_space=pltpu.VMEM)
ANY = pl.BlockSpec(memory_space=pl.ANY)
SMEM = pl.BlockSpec(memory_space=pltpu.SMEM)
ROOM = pltpu.CompilerParams(vmem_limit_bytes=48 * 1024 * 1024)


def across_chip():
    return [(r, r ^ 1) for r in range(2 * ZH)]


def along_z(d):
    return [(r, ((r // 2 + d) % ZH) * 2 + r % 2) for r in range(2 * ZH)]


def swap_zy():
    pairs = []
    for z in range(ZH):
        for c in range(2):
            for y in range(Y):
                for x in range(X):
                    goal = ((y * 2 + c) * Y + z) * X + (x ^ (2 * c))
                    pairs.append((((z * 2 + c) * Y + y) * X + x, goal))
    return pairs


def exchange(m):
    return [(f, f ^ m) for f in range(Y * X)]


def cost(us):
    return pl.CostEstimate(flops=0, bytes_accessed=us * 3600000, transcendentals=0)


def iota(shape, axis):
    return lax.broadcasted_iota(i32, shape, axis)


def attention_kernel(
    lengths, q, keys, values, nk, nv, out, q_wide, q_rows, fresh, o_rows, ck, cv, arrival
):
    steps, seqs, width = q.shape
    cached = ck.shape[1]
    kv_heads = ck.shape[2] // HD
    group = width // (kv_heads * HD)
    rows = group * steps
    scale = HD ** (-0.5)
    copies = [
        [
            pltpu.make_async_copy(whole.at[b], held.at[b], arrival.at[i, b])
            for i, (whole, held) in enumerate(((keys, ck), (values, cv)))
        ]
        for b in range(seqs)
    ]
    for pair in copies:
        for copy in pair:
            copy.start()
    q_wide[...] = q[...].astype(f32)
    fresh[...] = jnp.zeros_like(fresh)
    place = iota((rows, cached), 1)
    fresh_place = iota((rows, HD), 1)
    live_fresh = fresh_place <= iota((rows, HD), 0) % steps
    for b in range(seqs):
        live = place < lengths[b]
        for copy in copies[b]:
            copy.wait()
        for k in range(kv_heads):
            lanes = pl.ds(k * HD, HD)
            for g in range(group):
                q_rows[pl.ds(g * steps, steps), :] = q_wide[
                    :, b, pl.ds((k * group + g) * HD, HD)
                ]
            for j in range(steps):
                fresh[0, pl.ds(j, 1), :] = nk[j, pl.ds(b, 1), lanes].astype(f32)
                fresh[1, pl.ds(j, 1), :] = nv[j, pl.ds(b, 1), lanes].astype(f32)
            rows_q = q_rows[...].astype(bf16)
            old = lax.dot_general(rows_q, ck[b, :, lanes], NT, preferred_element_type=f32) * scale
            new = (
                lax.dot_general(rows_q, fresh[0].astype(bf16), NT, preferred_element_type=f32) * scale
            )
            old = jnp.where(live, old, -jnp.inf)
            new = jnp.where(live_fresh, new, -jnp.inf)
            top = jnp.maximum(
                jnp.max(old, axis=1, keepdims=True), jnp.max(new, axis=1, keepdims=True)
            )
            old = jnp.exp(old - top)
            new = jnp.exp(new - top)
            share = 1.0 / (
                jnp.sum(old, axis=1, keepdims=True) + jnp.sum(new, axis=1, keepdims=True)
            )
            mixed = jnp.dot(
                (old * share).astype(bf16), cv[b, :, lanes], preferred_element_type=f32
            ) + jnp.dot(
                (new * share).astype(bf16), fresh[1].astype(bf16), preferred_element_type=f32
            )
            for g in range(group):
                o_rows[pl.ds(b * steps, steps), pl.ds((k * group + g) * HD, HD)] = mixed[
                    g * steps : (g + 1) * steps, :
                ]
    done = o_rows[...].astype(bf16)
    for f in range(out.shape[0]):
        out[f] = done


def attention(lengths, q, ck, cv, nk, nv, copies):
    steps, seqs, width = q.shape
    rows = steps * seqs
    group = width // ck.shape[2]
    return pl.pallas_call(
        attention_kernel,
        out_shape=jax.ShapeDtypeStruct((copies, rows, width), bf16),
        in_specs=[SMEM, VMEM, ANY, ANY, VMEM, VMEM],
        out_specs=VMEM,
        scratch_shapes=[
            pltpu.VMEM((steps, seqs, width), f32),
            pltpu.VMEM((group * steps, HD), f32),
            pltpu.VMEM((2, HD, HD), f32),
            pltpu.VMEM((rows, width), f32),
            pltpu.VMEM(ck.shape, bf16),
            pltpu.VMEM(cv.shape, bf16),
            pltpu.SemaphoreType.DMA((2, seqs)),
        ],
        compiler_params=ROOM,
        cost_estimate=cost(7),
        name="attention",
    )(lengths, q, ck, cv, nk, nv)


def project_kernel(place, attn, mine, theirs, out):
    rows, width = out.shape
    steps = 4
    depth = mine.shape[1]
    total = jnp.zeros((rows, width), f32)
    for d in range(ZH):
        for same, held in ((True, mine), (False, theirs)):
            z = lax.rem(place[0] + ZH - d, ZH)
            r = 2 * z + (place[1] if same else 1 - place[1])
            columns = pl.ds(pl.multiple_of(r * depth, depth), depth)
            total = total + jnp.dot(attn[:, columns], held[d], preferred_element_type=f32)
    by_step = jnp.swapaxes(total.reshape(rows // steps, steps, width), 0, 1)
    out[...] = by_step.reshape(rows, width).astype(bf16)


def project(place, attn, mine, theirs):
    return pl.pallas_call(
        project_kernel,
        out_shape=jax.ShapeDtypeStruct((attn.shape[0], mine.shape[2]), bf16),
        in_specs=[SMEM] + [VMEM] * 3,
        out_specs=VMEM,
        compiler_params=ROOM,
        cost_estimate=cost(3),
        name="project",
    )(place, attn, mine, theirs)


def dispatch_kernel(ids, scaled, out):
    experts, slots, _ = out.shape
    top, rows = ids.shape
    block = rows // (slots // CAP)
    expert = iota((experts, rows), 0)
    hit = jnp.zeros((experts, rows), jnp.bool_)
    for k in range(top):
        hit = hit | (ids[pl.ds(k, 1), :] == expert)
    before, after = iota((rows, rows), 0), iota((rows, rows), 1)
    earlier = (before <= after) & (before // block == after // block)
    rank = jnp.dot(
        hit.astype(f32).astype(bf16), earlier.astype(f32).astype(bf16), preferred_element_type=f32
    ).astype(i32)
    slot_of = jnp.where(hit, iota((experts, rows), 1) // block * CAP + rank - 1, -1)
    slot = iota((slots, rows), 0)
    for e in range(experts):
        pick = jnp.where(slot_of[e : e + 1, :] == slot, f32(1.0), f32(0.0)).astype(bf16)
        out[e] = jnp.dot(pick, scaled[...], preferred_element_type=f32).astype(bf16)


def dispatch(ids, scaled, experts, steps):
    return pl.pallas_call(
        dispatch_kernel,
        out_shape=jax.ShapeDtypeStruct((experts, steps * CAP, scaled.shape[1]), bf16),
        in_specs=[VMEM] * 2,
        out_specs=VMEM,
        compiler_params=ROOM,
        cost_estimate=cost(2),
        name="dispatch",
    )(ids, scaled)


def expand_rows(place, arrived, near, far, ahead):
    total = None
    for i in range(4):
        held = (near, far)[i // 2][i % 2]
        rows = jnp.concatenate([arrived[4 * lax.rem(place[0] + d, ZH) + i] for d in ahead])
        part = jnp.dot(rows, held, preferred_element_type=f32)
        total = part if total is None else total + part
    return total


def expand_far_kernel(place, arrived, near, far, low, high):
    total = expand_rows(place, arrived, near, far, (2,))
    half = total.shape[0] // 2
    low[...] = total[:half].astype(bf16)
    high[...] = total[half:].astype(bf16)


def expand_near_kernel(place, arrived, near, far, plus, plus_ready, minus_ready, minus, own):
    total = expand_rows(place, arrived, near, far, (1, 3, 0))
    half = plus.shape[0]
    for i, out in enumerate((plus, plus_ready, minus_ready, minus)):
        out[...] = total[i * half : (i + 1) * half].astype(out.dtype)
    own[...] = total[4 * half :]


def expand_far(place, arrived, near, far):
    half, width = arrived.shape[1] // 2, near.shape[2]
    return pl.pallas_call(
        expand_far_kernel,
        out_shape=[jax.ShapeDtypeStruct((half, width), bf16)] * 2,
        in_specs=[SMEM] + [VMEM] * 3,
        out_specs=[VMEM] * 2,
        compiler_params=ROOM,
        cost_estimate=cost(2),
        name="expand_far",
    )(place, arrived, near, far)


def expand_near(place, arrived, near, far):
    slots, width = arrived.shape[1], near.shape[2]
    return pl.pallas_call(
        expand_near_kernel,
        out_shape=[
            jax.ShapeDtypeStruct((slots // 2, width), kind) for kind in (f32, bf16, bf16, f32)
        ]
        + [jax.ShapeDtypeStruct((slots, width), f32)],
        in_specs=[SMEM] + [VMEM] * 3,
        out_specs=[VMEM] * 5,
        compiler_params=ROOM,
        cost_estimate=cost(4),
        name="expand_near",
    )(place, arrived, near, far)


def contract_kernel(
    steps,
    place,
    ids,
    squares,
    own,
    plus,
    plus_ready,
    minus_ready,
    minus,
    first,
    second,
    out,
    upper,
    lower,
    arrival,
):
    copies = [
        [
            pltpu.make_async_copy(whole.at[r], held.at[r], arrival.at[i, r])
            for i, (whole, held) in enumerate(((first, upper), (second, lower)))
        ]
        for r in range(first.shape[0])
    ]
    for pair in copies:
        for copy in pair:
            copy.start()
    slots, width = out.shape[1:]
    half = own.shape[1] // 2
    top, rows = ids.shape
    block = rows // steps
    total = jnp.sum(squares[...], axis=0, keepdims=True)
    row_scale = lax.rsqrt(total / D + norm_eps)
    hit = jnp.zeros((8, rows), jnp.bool_)
    for k in range(top):
        hit = hit | (jnp.broadcast_to(ids[pl.ds(k, 1), :], (8, rows)) == place[2])
    before, after = iota((rows, rows), 0), iota((rows, rows), 1)
    earlier = (before <= after) & (before // block == after // block)
    rank = jnp.dot(
        hit.astype(f32).astype(bf16), earlier.astype(f32).astype(bf16), preferred_element_type=f32
    ).astype(i32)
    slot_of = jnp.where(hit, iota((8, rows), 1) // block * CAP + rank - 1, -1)
    pick = slot_of[0:1, :] == iota((slots, rows), 0)
    slot_scale = jnp.sum(jnp.where(pick, row_scale, 0.0), axis=1, keepdims=True)
    sums = [
        first[...].astype(f32) + second[...].astype(f32)
        for first, second in ((plus, minus_ready), (plus_ready, minus))
    ]
    both = (own[...] + jnp.concatenate(sums)) * slot_scale
    gate, up = both[:, :half], both[:, half:]
    hidden = (gate / (1.0 + jnp.exp(-gate)) * up).astype(bf16)
    split = half // 2
    for r, pair in enumerate(copies):
        for copy in pair:
            copy.wait()
        result = jnp.dot(hidden[:, :split], upper[r], preferred_element_type=f32)
        result = result + jnp.dot(hidden[:, split:], lower[r], preferred_element_type=f32)
        for i in range(2):
            out[2 * r + i] = result[:, i * width : (i + 1) * width].astype(bf16)


def contract(steps, place, ids, squares, parts, weights, experts, width):
    slots = parts[0].shape[0]
    return pl.pallas_call(
        functools.partial(contract_kernel, steps),
        out_shape=jax.ShapeDtypeStruct((experts, slots, width), bf16),
        in_specs=[SMEM] + [VMEM] * (2 + len(parts)) + [ANY] * 2,
        out_specs=VMEM,
        scratch_shapes=[
            pltpu.VMEM(weights[0].shape, bf16),
            pltpu.VMEM(weights[1].shape, bf16),
            pltpu.SemaphoreType.DMA((2, weights[0].shape[0])),
        ],
        compiler_params=ROOM,
        cost_estimate=cost(5),
        name="contract",
    )(place, ids, squares, *parts, *weights)


def combine_kernel(steps, ids, gates, *refs):
    *returned, out = refs
    experts, slots, _ = returned[0].shape
    rows, top = ids.shape
    block = rows // steps
    expert = iota((rows, experts), 1)
    hit = jnp.zeros((rows, experts), jnp.bool_)
    gate = jnp.zeros((rows, experts), f32)
    wide_gates = gates[...].astype(f32)
    for k in range(top):
        named = ids[:, k : k + 1] == expert
        hit = hit | named
        gate = jnp.where(named, wide_gates[:, k : k + 1], gate)
    after, before = iota((rows, rows), 0), iota((rows, rows), 1)
    earlier = (before <= after) & (before // block == after // block)
    rank = jnp.dot(
        earlier.astype(f32).astype(bf16), hit.astype(f32).astype(bf16), preferred_element_type=f32
    ).astype(i32)
    slot_of = jnp.where(hit, iota((rows, experts), 0) // block * CAP + rank - 1, -1)
    part = rows // len(returned)
    for i, held in enumerate(returned):
        slot = iota((part, slots), 1) + i * slots
        total = jnp.zeros((part, out.shape[1]), f32)
        of, by = slot_of[i * part : (i + 1) * part], gate[i * part : (i + 1) * part]
        for e in range(experts):
            weights = jnp.where(of[:, e : e + 1] == slot, by[:, e : e + 1], 0.0).astype(bf16)
            total = total + jnp.dot(weights, held[e], preferred_element_type=f32)
        out[pl.ds(i * part, part), :] = total.astype(bf16)


def combine(steps, ids, gates, returned):
    return pl.pallas_call(
        functools.partial(combine_kernel, steps),
        out_shape=jax.ShapeDtypeStruct((ids.shape[0], returned[0].shape[2]), bf16),
        in_specs=[VMEM] * (2 + len(returned)),
        out_specs=VMEM,
        compiler_params=ROOM,
        cost_estimate=cost(2),
        name="combine",
    )(ids, gates, *returned)


def on_device(
    queries,
    cache_keys,
    cache_values,
    new_keys,
    new_values,
    lengths,
    attn_out_weight,
    residual,
    norm_gain,
    expert_ids,
    gate_weights,
    expert_in,
    expert_out,
):
    rep, fsdp = lax.axis_index("rep"), lax.axis_index("fsdp")
    z, c = rep // 2, rep % 2
    place = jnp.stack([z, c, fsdp, lax.axis_index("tp")]).astype(i32)
    steps, block, top = expert_ids.shape
    experts = Y * X
    rows, model = steps * block, residual.shape[2]
    ids_by_step = expert_ids.reshape(rows, top)
    ids_across = jnp.transpose(ids_by_step)

    def shift(value, d):
        return lax.ppermute(value, "rep", along_z(d))

    def core(value):
        return lax.ppermute(value, "rep", across_chip())

    proj_minus, proj_plus = shift(attn_out_weight, 1), shift(attn_out_weight, -1)
    ids_there = lax.ppermute(ids_across, PLACES, swap_zy())
    attn = attention(lengths, queries, cache_keys, cache_values, new_keys, new_values, experts)
    quarter = expert_out.shape[1] // 2
    out_first, out_second = expert_out[0, :quarter], expert_out[0, quarter:]
    attn, ids_there, proj_minus, proj_plus, out_first = lax.optimization_barrier(
        (attn, ids_there, proj_minus, proj_plus, out_first)
    )
    out_first = lax.all_gather(out_first, "rep", axis=0, tiled=False)
    split = proj_minus.shape[0] // 2
    proj_far = [shift(proj_minus[:split], 1), shift(proj_plus[split:], -1)]

    near_in = expert_in[0].reshape(expert_in.shape[1], -1)
    attn, near_in = lax.optimization_barrier((attn, near_in))
    far_in = core(near_in)
    attn = lax.all_to_all(attn, "fsdp", split_axis=0, concat_axis=0, tiled=True)
    mine = jnp.stack([attn_out_weight, proj_minus, jnp.concatenate(proj_far), proj_plus])
    attn, mine, theirs = lax.optimization_barrier((attn, mine, core(mine)))
    near_in, far_in = near_in.reshape(2, model, -1), far_in.reshape(2, model, -1)
    partial = project(place, attn.reshape(rows, -1), mine, theirs)
    here_cross = lax.ppermute(partial, "tp", OTHER_HALF)
    attended = residual.astype(f32).reshape(rows, model) + (
        partial.astype(f32) + here_cross.astype(f32)
    )
    scaled = (attended * norm_gain).astype(bf16)
    there = lax.ppermute(scaled, PLACES, swap_zy())

    squares = jnp.sum(attended * attended, axis=-1).reshape(1, rows)
    for m in (1, 2):
        squares = squares + lax.ppermute(squares, "fsdp", exchange(m))

    there, out_second, squares = lax.optimization_barrier((there, out_second, squares))
    out_second = lax.all_gather(out_second, "rep", axis=0, tiled=False)
    dispatched = dispatch(ids_there, there, experts, steps)
    arrived = lax.all_to_all(dispatched, "fsdp", split_axis=0, concat_axis=0, tiled=True)

    for m in (4, 8):
        squares = squares + lax.ppermute(squares, "fsdp", exchange(m))
    arrived, squares = lax.optimization_barrier((arrived, squares))

    low, high = expand_far(place, arrived, near_in, far_in)
    low, high = shift(low, 1), shift(high, -1)
    plus, plus_ready, minus_ready, minus, own = expand_near(place, arrived, near_in, far_in)
    plus_ready, minus_ready = shift(plus_ready, 1), shift(minus_ready, -1)
    low, high, plus, minus = lax.optimization_barrier((low, high, plus, minus))
    plus = (plus + low.astype(f32)).astype(bf16)
    minus = (minus + high.astype(f32)).astype(bf16)
    plus, minus = shift(plus, 1), shift(minus, -1)

    result = contract(
        steps,
        place,
        ids_across,
        squares,
        [own, plus, plus_ready, minus_ready, minus],
        [out_first, out_second],
        experts,
        model,
    )
    returned = lax.all_to_all(result, "fsdp", split_axis=0, concat_axis=0, tiled=True)
    routed = combine(steps, ids_by_step, gate_weights.reshape(rows, top), [returned])
    routed_cross = lax.ppermute(routed, "tp", OTHER_HALF)
    routed = routed.astype(f32) + routed_cross.astype(f32)
    return (attended + routed).astype(bf16).reshape(steps, block, model)


def solution(mesh):
    placed = (
        P(None, ("rep", "fsdp"), "tp"),
        P(("rep", "fsdp"), None, "tp"),
        P(("rep", "fsdp"), None, "tp"),
        P(None, ("rep", "fsdp"), "tp"),
        P(None, ("rep", "fsdp"), "tp"),
        P(("rep", "fsdp")),
        P(("tp", "rep"), "fsdp"),
        P(None, "rep", "fsdp"),
        P("fsdp"),
        P(None, "rep", None),
        P(None, "rep", None),
        P("fsdp", "rep", None, "tp"),
        P("fsdp", "tp", "rep"),
    )
    return jax.shard_map(
        on_device, mesh=mesh, in_specs=placed, out_specs=P(None, "rep", "fsdp"), check_vma=False
    )
```

```python
import functools

import jax
import jax.numpy as jnp
from jax import lax
from jax.experimental import pallas as pl
from jax.experimental.pallas import tpu as pltpu
from jax.sharding import PartitionSpec as P

D = 4096
HD = 128
ZH, Y, X = 4, 4, 4
CAP = 48
PLACES = ("rep", "fsdp")
OTHER_HALF = [(0, 1), (1, 0)]
norm_eps = 1e-06
bf16 = jnp.bfloat16
f32 = jnp.float32
i32 = jnp.int32
NT = (((1,), (1,)), ((), ()))
VMEM = pl.BlockSpec(memory_space=pltpu.VMEM)
ANY = pl.BlockSpec(memory_space=pl.ANY)
SMEM = pl.BlockSpec(memory_space=pltpu.SMEM)
ROOM = pltpu.CompilerParams(vmem_limit_bytes=48 * 1024 * 1024)


def across_chip():
    return [(r, r ^ 1) for r in range(2 * ZH)]


def along_z(d):
    return [(r, ((r // 2 + d) % ZH) * 2 + r % 2) for r in range(2 * ZH)]


def swap_zy():
    pairs = []
    for z in range(ZH):
        for c in range(2):
            for y in range(Y):
                for x in range(X):
                    goal = ((y * 2 + c) * Y + z) * X + (x ^ (2 * c))
                    pairs.append((((z * 2 + c) * Y + y) * X + x, goal))
    return pairs


def exchange(m):
    return [(f, f ^ m) for f in range(Y * X)]


def cost(us):
    return pl.CostEstimate(flops=0, bytes_accessed=us * 3600000, transcendentals=0)


def iota(shape, axis):
    return lax.broadcasted_iota(i32, shape, axis)


def attention_kernel(
    lengths, q, keys, values, nk, nv, out, q_wide, q_rows, fresh, o_rows, ck, cv, arrival
):
    steps, seqs, width = q.shape
    cached = ck.shape[1]
    kv_heads = ck.shape[2] // HD
    group = width // (kv_heads * HD)
    rows = group * steps
    scale = HD ** (-0.5)
    copies = [
        [
            pltpu.make_async_copy(whole.at[b], held.at[b], arrival.at[i, b])
            for i, (whole, held) in enumerate(((keys, ck), (values, cv)))
        ]
        for b in range(seqs)
    ]
    for pair in copies:
        for copy in pair:
            copy.start()
    q_wide[...] = q[...].astype(f32)
    fresh[...] = jnp.zeros_like(fresh)
    place = iota((rows, cached), 1)
    fresh_place = iota((rows, HD), 1)
    live_fresh = fresh_place <= iota((rows, HD), 0) % steps
    for b in range(seqs):
        live = place < lengths[b]
        for copy in copies[b]:
            copy.wait()
        for k in range(kv_heads):
            lanes = pl.ds(k * HD, HD)
            for g in range(group):
                q_rows[pl.ds(g * steps, steps), :] = q_wide[
                    :, b, pl.ds((k * group + g) * HD, HD)
                ]
            for j in range(steps):
                fresh[0, pl.ds(j, 1), :] = nk[j, pl.ds(b, 1), lanes].astype(f32)
                fresh[1, pl.ds(j, 1), :] = nv[j, pl.ds(b, 1), lanes].astype(f32)
            rows_q = q_rows[...].astype(bf16)
            old = lax.dot_general(rows_q, ck[b, :, lanes], NT, preferred_element_type=f32) * scale
            new = (
                lax.dot_general(rows_q, fresh[0].astype(bf16), NT, preferred_element_type=f32) * scale
            )
            old = jnp.where(live, old, -jnp.inf)
            new = jnp.where(live_fresh, new, -jnp.inf)
            top = jnp.maximum(
                jnp.max(old, axis=1, keepdims=True), jnp.max(new, axis=1, keepdims=True)
            )
            old = jnp.exp(old - top)
            new = jnp.exp(new - top)
            share = 1.0 / (
                jnp.sum(old, axis=1, keepdims=True) + jnp.sum(new, axis=1, keepdims=True)
            )
            mixed = jnp.dot(
                (old * share).astype(bf16), cv[b, :, lanes], preferred_element_type=f32
            ) + jnp.dot(
                (new * share).astype(bf16), fresh[1].astype(bf16), preferred_element_type=f32
            )
            for g in range(group):
                o_rows[pl.ds(b * steps, steps), pl.ds((k * group + g) * HD, HD)] = mixed[
                    g * steps : (g + 1) * steps, :
                ]
    done = o_rows[...].astype(bf16)
    for f in range(out.shape[0]):
        out[f] = done


def attention(lengths, q, ck, cv, nk, nv, copies):
    steps, seqs, width = q.shape
    rows = steps * seqs
    group = width // ck.shape[2]
    return pl.pallas_call(
        attention_kernel,
        out_shape=jax.ShapeDtypeStruct((copies, rows, width), bf16),
        in_specs=[SMEM, VMEM, ANY, ANY, VMEM, VMEM],
        out_specs=VMEM,
        scratch_shapes=[
            pltpu.VMEM((steps, seqs, width), f32),
            pltpu.VMEM((group * steps, HD), f32),
            pltpu.VMEM((2, HD, HD), f32),
            pltpu.VMEM((rows, width), f32),
            pltpu.VMEM(ck.shape, bf16),
            pltpu.VMEM(cv.shape, bf16),
            pltpu.SemaphoreType.DMA((2, seqs)),
        ],
        compiler_params=ROOM,
        cost_estimate=cost(7),
        name="attention",
    )(lengths, q, ck, cv, nk, nv)


def project_kernel(place, attn, mine, theirs, out):
    rows, width = out.shape
    steps = 4
    depth = mine.shape[1]
    total = jnp.zeros((rows, width), f32)
    for d in range(ZH):
        for same, held in ((True, mine), (False, theirs)):
            z = lax.rem(place[0] + ZH - d, ZH)
            r = 2 * z + (place[1] if same else 1 - place[1])
            columns = pl.ds(pl.multiple_of(r * depth, depth), depth)
            total = total + jnp.dot(attn[:, columns], held[d], preferred_element_type=f32)
    by_step = jnp.swapaxes(total.reshape(rows // steps, steps, width), 0, 1)
    out[...] = by_step.reshape(rows, width).astype(bf16)


def project(place, attn, mine, theirs):
    return pl.pallas_call(
        project_kernel,
        out_shape=jax.ShapeDtypeStruct((attn.shape[0], mine.shape[2]), bf16),
        in_specs=[SMEM] + [VMEM] * 3,
        out_specs=VMEM,
        compiler_params=ROOM,
        cost_estimate=cost(3),
        name="project",
    )(place, attn, mine, theirs)


def dispatch_kernel(ids, scaled, out):
    experts, slots, _ = out.shape
    top, rows = ids.shape
    block = rows // (slots // CAP)
    expert = iota((experts, rows), 0)
    hit = jnp.zeros((experts, rows), jnp.bool_)
    for k in range(top):
        hit = hit | (ids[pl.ds(k, 1), :] == expert)
    before, after = iota((rows, rows), 0), iota((rows, rows), 1)
    earlier = (before <= after) & (before // block == after // block)
    rank = jnp.dot(
        hit.astype(f32).astype(bf16), earlier.astype(f32).astype(bf16), preferred_element_type=f32
    ).astype(i32)
    slot_of = jnp.where(hit, iota((experts, rows), 1) // block * CAP + rank - 1, -1)
    slot = iota((slots, rows), 0)
    for e in range(experts):
        pick = jnp.where(slot_of[e : e + 1, :] == slot, f32(1.0), f32(0.0)).astype(bf16)
        out[e] = jnp.dot(pick, scaled[...], preferred_element_type=f32).astype(bf16)


def dispatch(ids, scaled, experts, steps):
    return pl.pallas_call(
        dispatch_kernel,
        out_shape=jax.ShapeDtypeStruct((experts, steps * CAP, scaled.shape[1]), bf16),
        in_specs=[VMEM] * 2,
        out_specs=VMEM,
        compiler_params=ROOM,
        cost_estimate=cost(2),
        name="dispatch",
    )(ids, scaled)


def expand_rows(place, arrived, near, far, ahead):
    total = None
    for i in range(4):
        held = (near, far)[i // 2][i % 2]
        rows = jnp.concatenate([arrived[4 * lax.rem(place[0] + d, ZH) + i] for d in ahead])
        part = jnp.dot(rows, held, preferred_element_type=f32)
        total = part if total is None else total + part
    return total


def expand_far_kernel(place, arrived, near, far, low, high):
    total = expand_rows(place, arrived, near, far, (2,))
    half = total.shape[0] // 2
    low[...] = total[:half].astype(bf16)
    high[...] = total[half:].astype(bf16)


def expand_near_kernel(place, arrived, near, far, plus, plus_ready, minus_ready, minus, own):
    total = expand_rows(place, arrived, near, far, (1, 3, 0))
    half = plus.shape[0]
    for i, out in enumerate((plus, plus_ready, minus_ready, minus)):
        out[...] = total[i * half : (i + 1) * half].astype(out.dtype)
    own[...] = total[4 * half :]


def expand_far(place, arrived, near, far):
    half, width = arrived.shape[1] // 2, near.shape[2]
    return pl.pallas_call(
        expand_far_kernel,
        out_shape=[jax.ShapeDtypeStruct((half, width), bf16)] * 2,
        in_specs=[SMEM] + [VMEM] * 3,
        out_specs=[VMEM] * 2,
        compiler_params=ROOM,
        cost_estimate=cost(2),
        name="expand_far",
    )(place, arrived, near, far)


def expand_near(place, arrived, near, far):
    slots, width = arrived.shape[1], near.shape[2]
    return pl.pallas_call(
        expand_near_kernel,
        out_shape=[
            jax.ShapeDtypeStruct((slots // 2, width), kind) for kind in (f32, bf16, bf16, f32)
        ]
        + [jax.ShapeDtypeStruct((slots, width), f32)],
        in_specs=[SMEM] + [VMEM] * 3,
        out_specs=[VMEM] * 5,
        compiler_params=ROOM,
        cost_estimate=cost(4),
        name="expand_near",
    )(place, arrived, near, far)


def contract_kernel(
    steps,
    place,
    ids,
    squares,
    *refs,
):
    sent, (first, second, out), held_parts = refs[:5], refs[5:8], refs[8:13]
    upper, lower, arrival, part_arrival = refs[13:]
    own, plus, plus_ready, minus_ready, minus = held_parts
    part_copies = [
        pltpu.make_async_copy(whole, held, part_arrival.at[i])
        for i, (whole, held) in enumerate(zip(sent, held_parts))
    ]
    for copy in part_copies:
        copy.start()
    copies = [
        [
            pltpu.make_async_copy(whole.at[r], held.at[r], arrival.at[i, r])
            for i, (whole, held) in enumerate(((first, upper), (second, lower)))
        ]
        for r in range(first.shape[0])
    ]
    for pair in copies:
        for copy in pair:
            copy.start()
    slots, width = out.shape[1:]
    half = own.shape[1] // 2
    top, rows = ids.shape
    block = rows // steps
    total = jnp.sum(squares[...], axis=0, keepdims=True)
    row_scale = lax.rsqrt(total / D + norm_eps)
    hit = jnp.zeros((8, rows), jnp.bool_)
    for k in range(top):
        hit = hit | (jnp.broadcast_to(ids[pl.ds(k, 1), :], (8, rows)) == place[2])
    before, after = iota((rows, rows), 0), iota((rows, rows), 1)
    earlier = (before <= after) & (before // block == after // block)
    rank = jnp.dot(
        hit.astype(f32).astype(bf16), earlier.astype(f32).astype(bf16), preferred_element_type=f32
    ).astype(i32)
    slot_of = jnp.where(hit, iota((8, rows), 1) // block * CAP + rank - 1, -1)
    pick = slot_of[0:1, :] == iota((slots, rows), 0)
    slot_scale = jnp.sum(jnp.where(pick, row_scale, 0.0), axis=1, keepdims=True)
    for copy in part_copies:
        copy.wait()
    sums = [
        one[...].astype(f32) + two[...].astype(f32)
        for one, two in ((plus, minus_ready), (plus_ready, minus))
    ]
    both = (own[...] + jnp.concatenate(sums)) * slot_scale
    gate, up = both[:, :half], both[:, half:]
    hidden = (gate / (1.0 + jnp.exp(-gate)) * up).astype(bf16)
    split = half // 2
    for r, pair in enumerate(copies):
        for copy in pair:
            copy.wait()
        result = jnp.dot(hidden[:, :split], upper[r], preferred_element_type=f32)
        result = result + jnp.dot(hidden[:, split:], lower[r], preferred_element_type=f32)
        for i in range(2):
            out[2 * r + i] = result[:, i * width : (i + 1) * width].astype(bf16)


def contract(steps, place, ids, squares, parts, weights, experts, width):
    slots = parts[0].shape[0]
    return pl.pallas_call(
        functools.partial(contract_kernel, steps),
        out_shape=jax.ShapeDtypeStruct((experts, slots, width), bf16),
        in_specs=[SMEM] + [VMEM] * 2 + [ANY] * (len(parts) + 2),
        out_specs=VMEM,
        scratch_shapes=[pltpu.VMEM(part.shape, part.dtype) for part in parts]
        + [
            pltpu.VMEM(weights[0].shape, bf16),
            pltpu.VMEM(weights[1].shape, bf16),
            pltpu.SemaphoreType.DMA((2, weights[0].shape[0])),
            pltpu.SemaphoreType.DMA((len(parts),)),
        ],
        compiler_params=ROOM,
        cost_estimate=cost(5),
        name="contract",
    )(place, ids, squares, *parts, *weights)


def combine_kernel(steps, ids, gates, *refs):
    *returned, out = refs
    experts, slots, _ = returned[0].shape
    rows, top = ids.shape
    block = rows // steps
    expert = iota((rows, experts), 1)
    hit = jnp.zeros((rows, experts), jnp.bool_)
    gate = jnp.zeros((rows, experts), f32)
    wide_gates = gates[...].astype(f32)
    for k in range(top):
        named = ids[:, k : k + 1] == expert
        hit = hit | named
        gate = jnp.where(named, wide_gates[:, k : k + 1], gate)
    after, before = iota((rows, rows), 0), iota((rows, rows), 1)
    earlier = (before <= after) & (before // block == after // block)
    rank = jnp.dot(
        earlier.astype(f32).astype(bf16), hit.astype(f32).astype(bf16), preferred_element_type=f32
    ).astype(i32)
    slot_of = jnp.where(hit, iota((rows, experts), 0) // block * CAP + rank - 1, -1)
    part = rows // len(returned)
    for i, held in enumerate(returned):
        slot = iota((part, slots), 1) + i * slots
        total = jnp.zeros((part, out.shape[1]), f32)
        of, by = slot_of[i * part : (i + 1) * part], gate[i * part : (i + 1) * part]
        for e in range(experts):
            weights = jnp.where(of[:, e : e + 1] == slot, by[:, e : e + 1], 0.0).astype(bf16)
            total = total + jnp.dot(weights, held[e], preferred_element_type=f32)
        out[pl.ds(i * part, part), :] = total.astype(bf16)


def combine(steps, ids, gates, returned):
    return pl.pallas_call(
        functools.partial(combine_kernel, steps),
        out_shape=jax.ShapeDtypeStruct((ids.shape[0], returned[0].shape[2]), bf16),
        in_specs=[VMEM] * (2 + len(returned)),
        out_specs=VMEM,
        compiler_params=ROOM,
        cost_estimate=cost(2),
        name="combine",
    )(ids, gates, *returned)


def on_device(
    queries,
    cache_keys,
    cache_values,
    new_keys,
    new_values,
    lengths,
    attn_out_weight,
    residual,
    norm_gain,
    expert_ids,
    gate_weights,
    expert_in,
    expert_out,
):
    rep, fsdp = lax.axis_index("rep"), lax.axis_index("fsdp")
    z, c = rep // 2, rep % 2
    place = jnp.stack([z, c, fsdp, lax.axis_index("tp")]).astype(i32)
    steps, block, top = expert_ids.shape
    experts = Y * X
    rows, model = steps * block, residual.shape[2]
    ids_by_step = expert_ids.reshape(rows, top)
    ids_across = jnp.transpose(ids_by_step)

    def shift(value, d):
        return lax.ppermute(value, "rep", along_z(d))

    def core(value):
        return lax.ppermute(value, "rep", across_chip())

    proj_minus, proj_plus = shift(attn_out_weight, 1), shift(attn_out_weight, -1)
    ids_there = lax.ppermute(ids_across, PLACES, swap_zy())
    attn = attention(lengths, queries, cache_keys, cache_values, new_keys, new_values, experts)
    quarter = expert_out.shape[1] // 2
    out_first, out_second = expert_out[0, :quarter], expert_out[0, quarter:]
    attn, ids_there, proj_minus, proj_plus, out_first = lax.optimization_barrier(
        (attn, ids_there, proj_minus, proj_plus, out_first)
    )
    out_first = lax.all_gather(out_first, "rep", axis=0, tiled=False)
    split = proj_minus.shape[0] // 2
    proj_far = [shift(proj_minus[:split], 1), shift(proj_plus[split:], -1)]

    near_in = expert_in[0].reshape(expert_in.shape[1], -1)
    attn, near_in = lax.optimization_barrier((attn, near_in))
    far_in = core(near_in)
    attn = lax.all_to_all(attn, "fsdp", split_axis=0, concat_axis=0, tiled=True)
    mine = jnp.stack([attn_out_weight, proj_minus, jnp.concatenate(proj_far), proj_plus])
    attn, mine, theirs = lax.optimization_barrier((attn, mine, core(mine)))
    near_in, far_in = near_in.reshape(2, model, -1), far_in.reshape(2, model, -1)
    partial = project(place, attn.reshape(rows, -1), mine, theirs)
    here_cross = lax.ppermute(partial, "tp", OTHER_HALF)
    attended = residual.astype(f32).reshape(rows, model) + (
        partial.astype(f32) + here_cross.astype(f32)
    )
    scaled = (attended * norm_gain).astype(bf16)
    there = lax.ppermute(scaled, PLACES, swap_zy())

    squares = jnp.sum(attended * attended, axis=-1).reshape(1, rows)
    for m in (1, 2):
        squares = squares + lax.ppermute(squares, "fsdp", exchange(m))

    there, out_second, squares = lax.optimization_barrier((there, out_second, squares))
    out_second = lax.all_gather(out_second, "rep", axis=0, tiled=False)
    dispatched = dispatch(ids_there, there, experts, steps)
    arrived = lax.all_to_all(dispatched, "fsdp", split_axis=0, concat_axis=0, tiled=True)

    for m in (4, 8):
        squares = squares + lax.ppermute(squares, "fsdp", exchange(m))
    arrived, squares = lax.optimization_barrier((arrived, squares))

    low, high = expand_far(place, arrived, near_in, far_in)
    low, high = shift(low, 1), shift(high, -1)
    plus, plus_ready, minus_ready, minus, own = expand_near(place, arrived, near_in, far_in)
    plus_ready, minus_ready = shift(plus_ready, 1), shift(minus_ready, -1)
    low, high, plus, minus = lax.optimization_barrier((low, high, plus, minus))
    plus = (plus + low.astype(f32)).astype(bf16)
    minus = (minus + high.astype(f32)).astype(bf16)
    plus, minus = shift(plus, 1), shift(minus, -1)

    result = contract(
        steps,
        place,
        ids_across,
        squares,
        [own, plus, plus_ready, minus_ready, minus],
        [out_first, out_second],
        experts,
        model,
    )
    returned = lax.all_to_all(result, "fsdp", split_axis=0, concat_axis=0, tiled=True)
    routed = combine(steps, ids_by_step, gate_weights.reshape(rows, top), [returned])
    routed_cross = lax.ppermute(routed, "tp", OTHER_HALF)
    routed = routed.astype(f32) + routed_cross.astype(f32)
    return (attended + routed).astype(bf16).reshape(steps, block, model)


def solution(mesh):
    placed = (
        P(None, ("rep", "fsdp"), "tp"),
        P(("rep", "fsdp"), None, "tp"),
        P(("rep", "fsdp"), None, "tp"),
        P(None, ("rep", "fsdp"), "tp"),
        P(None, ("rep", "fsdp"), "tp"),
        P(("rep", "fsdp")),
        P(("tp", "rep"), "fsdp"),
        P(None, "rep", "fsdp"),
        P("fsdp"),
        P(None, "rep", None),
        P(None, "rep", None),
        P("fsdp", "rep", None, "tp"),
        P("fsdp", "tp", "rep"),
    )
    return jax.shard_map(
        on_device, mesh=mesh, in_specs=placed, out_specs=P(None, "rep", "fsdp"), check_vma=False
    )
```
